32 devices in a mesh: fsdp: 8 (over y, x, core), seq: 4 (over z).
Axes of the slice: x: 2, y: 2, z: 4, core: 2. Of those that a mesh axis runs over, the one named last changes fastest.
Arguments:
- normed: bfloat16 [256, 4096], P('fsdp', 'seq'), may hold values from -6 to 6
- doc_grads: bfloat16 [16, 4096], P('fsdp', 'seq'), may hold values from -96 to 96
- segment_ids: int32 [256], replicated, may hold values from 0 to 15, never falling along the last dimension, each value on 1 to 32 neighbouring positions
- w_gate: bfloat16 [4096, 12288], P('seq', 'fsdp'), may hold values from -0.09375 to 0.09375
- w_up: bfloat16 [4096, 12288], P('seq', 'fsdp'), may hold values from -0.09375 to 0.09375
- w_down: bfloat16 [12288, 4096], P('fsdp', 'seq'), may hold values from -0.0546875 to 0.0546875
Outputs:
- layer_out: bfloat16 [256, 4096], P('fsdp', 'seq')
- input_grad: bfloat16 [256, 4096], P('fsdp', 'seq')
- grad_gate: float32 [4096, 12288], P('seq', 'fsdp')
- grad_up: float32 [4096, 12288], P('seq', 'fsdp')
- grad_down: float32 [12288, 4096], P('fsdp', 'seq')
The draws below stay inside these ranges and needn't reach their ends.
Inputs may be any that keep to these rules, and one draw needn't show every extreme that they name: `segment_ids`: ids never fall along the tokens; each document has 1 to 32 tokens and one has exactly 32.
All inputs are finite; a program needn't handle non-finite values.
Results may differ from the reference program's by a relative error of at most 0.0051.
Values may be sent and summed in bfloat16 or wider, within the bound.
A program may use at most 128 MiB of HBM per device.

```python
import math
import jax
import jax.numpy as jnp
import numpy as np

D = 4096
FF = 12288
TOKENS = 256
DOCS = 16
MOST = 32


def levels(rng, shape, split, smallest, top_value):
    gain = 1.0
    for position, parts in split:
        heights = jax.random.uniform(jax.random.fold_in(jax.random.fold_in(rng, 6), position), (parts,), jnp.float32, smallest / len(split), top_value / len(split))
        gain = gain * jnp.repeat(jnp.exp(heights), shape[position] // parts).reshape((-1,) + (1,) * (len(shape) - 1 - position))
    return gain


def split_up(count, total, reach, lean):
    weights = [(1 << 20) // math.isqrt(standing ** lean) + 1 for standing in range(2, count + 1)]
    rest, given = total - reach - (count - 1), [1] * (count - 1)
    while rest > 0:
        candidates = [i for i in range(count - 1) if given[i] < reach]
        mass, budget = sum([weights[i] for i in candidates]), rest
        for i in candidates:
            addition = min(reach - given[i], max(1, budget * weights[i] // mass), rest)
            given[i] = given[i] + addition
            rest = rest - addition
    return np.array([reach] + given)


def uneven_parts(stream_key, amount, total, bound, slope):
    if amount == 2:
        one = jax.random.randint(stream_key, (), max(1, total - bound), min(bound, total - 1) + 1)
        return jnp.stack([one, total - one])
    tallies = jnp.asarray(split_up(amount, total, bound, slope), jnp.int32)
    pairs = (amount - 1) // 2
    donor, receiver = tallies[1:1 + 2 * pairs:2], tallies[2:2 + 2 * pairs:2]
    slack = jnp.minimum(donor - 1, bound - receiver)
    passed = jax.random.randint(jax.random.fold_in(stream_key, 1), (pairs,), 0, 1 << 20) % (slack + 1)
    tallies = tallies.at[1:1 + 2 * pairs:2].set(donor - passed).at[2:2 + 2 * pairs:2].set(receiver + passed)
    return tallies[jax.random.permutation(jax.random.fold_in(stream_key, 2), amount)]


def noise(rng, dims, spread, most, pieces=(), held_as=jnp.bfloat16):
    array = spread * jax.random.normal(rng, dims, jnp.float32)
    if pieces:
        array = array * levels(rng, dims, pieces, -0.22, 0.18)
    return jnp.clip(array, -most, most).astype(held_as)


def setup_inputs(seed: int = 0) -> dict:
    keys = jax.random.split(jax.random.key(seed), 7)
    normed = noise(keys[0], (TOKENS, D), 1.0, 6.0, ((0, 8), (1, 4)))
    doc_grads = noise(keys[1], (DOCS, D), (TOKENS // DOCS), 96.0, ((0, 8), (1, 4)))
    segment_ids = jnp.searchsorted(jnp.cumsum(uneven_parts(keys[2], DOCS, TOKENS, MOST, 2)), jnp.arange(TOKENS), side="right").astype(jnp.int32)
    w_gate = noise(keys[3], (D, FF), D ** -0.5, 0.09375, ((0, 4), (1, 8)))
    w_up = noise(keys[4], (D, FF), D ** -0.5, 0.09375, ((0, 4), (1, 8)))
    w_down = noise(keys[5], (FF, D), FF ** -0.5, 0.0546875, ((0, 8), (1, 4)))
    return dict(normed=normed, doc_grads=doc_grads, segment_ids=segment_ids, w_gate=w_gate, w_up=w_up, w_down=w_down)


def reference(normed, doc_grads, segment_ids, w_gate, w_up, w_down):
    gate = jnp.dot(normed, w_gate, preferred_element_type=jnp.float32)
    up = jnp.dot(normed, w_up, preferred_element_type=jnp.float32)
    sig = jax.nn.sigmoid(gate)
    hidden = (gate * sig * up).astype(jnp.bfloat16)
    layer_out = (normed.astype(jnp.float32) + jnp.dot(hidden, w_down, preferred_element_type=jnp.float32)).astype(jnp.bfloat16)
    matches = (segment_ids[:, None] == jnp.arange(DOCS, dtype=jnp.int32)[None, :]).astype(jnp.float32)
    counts = jnp.sum(matches, axis=0)
    per_doc = (doc_grads.astype(jnp.float32) / counts[:, None]).astype(jnp.bfloat16)
    out_grad = per_doc[segment_ids]
    grad_down = jnp.dot(hidden.T, out_grad, preferred_element_type=jnp.float32)
    hidden_grad = jnp.dot(out_grad, w_down.T, preferred_element_type=jnp.float32)
    gate_grad = (hidden_grad * up * sig * (1.0 + gate * (1.0 - sig))).astype(jnp.bfloat16)
    up_grad = (hidden_grad * gate * sig).astype(jnp.bfloat16)
    grad_gate = jnp.dot(normed.T, gate_grad, preferred_element_type=jnp.float32)
    grad_up = jnp.dot(normed.T, up_grad, preferred_element_type=jnp.float32)
    back = jnp.dot(gate_grad, w_gate.T, preferred_element_type=jnp.float32) + jnp.dot(up_grad, w_up.T, preferred_element_type=jnp.float32)
    input_grad = (out_grad.astype(jnp.float32) + back).astype(jnp.bfloat16)
    return layer_out, input_grad, grad_gate, grad_up, grad_down
```

```python
import functools

import jax
import jax.numpy as jnp
from jax import lax
from jax.experimental import pallas as pl
from jax.experimental.pallas import tpu as pltpu
from jax.sharding import PartitionSpec as P

MESH = pl.DeviceIdType.MESH
BF16, F32 = jnp.bfloat16, jnp.float32
VMEM_LIMIT = 52 * 1024 * 1024
NT = (((1,), (1,)), ((), ()))
TN = (((0,), (0,)), ((), ()))


def tile_of(width):
    return 256 if width % 256 == 0 else 128


def encoder_kernel(
    nf, ns, docs, piece_rows, doc_rows,
    normed_ref, doc_ref, seg_ref, wg_hbm, wu_hbm, wd_hbm,
    layer_ref, input_ref, rows_out, og_ref, hid_ref, gg_ref, ug_ref,
    wg_ref, wu_ref, wd_ref, rows_ref, docs_ref, own_ref, recv_l, recv_r, send_l, send_r,
    hg_own, hg_recv_l, hg_recv_r, hg_send_l, hg_send_r, hg_tok, rs_send, rs_recv, mine_ref,
    load_sems, ag_send, ag_recv, dg_send, dg_recv,
    r_send, r_recv, l_send, l_recv, hg_sems, rs_send_sems, rs_recv_sems,
):
    me, z = lax.axis_index("fsdp"), lax.axis_index("seq")
    t = normed_ref.shape[0]
    width = wg_ref.shape[1]
    feats = normed_ref.shape[1]
    ft = tile_of(width)
    has_left, has_right = z > 0, z < ns - 1
    low_half = z < ns // 2
    wire = send_l.dtype

    loads = [
        pltpu.make_async_copy(src, dst, load_sems.at[k])
        for k, (src, dst) in enumerate(((wd_hbm, wd_ref), (wg_hbm, wg_ref), (wu_hbm, wu_ref)))
    ]
    for load in loads:
        load.start()

    barrier = pltpu.get_barrier_semaphore()

    def greet(s, c):
        pl.semaphore_signal(barrier, inc=1, device_id=(lax.rem(me + 1 + s, nf), z), device_id_type=MESH)
        return c

    lax.fori_loop(0, nf - 1, greet, 0)

    @pl.when(has_left)
    def _():
        pl.semaphore_signal(barrier, inc=1, device_id=(me, z - 1), device_id_type=MESH)

    @pl.when(has_right)
    def _():
        pl.semaphore_signal(barrier, inc=1, device_id=(me, z + 1), device_id_type=MESH)

    rows_ref[me] = normed_ref[...]
    docs_ref[me] = doc_ref[...]

    @pl.when(jnp.logical_not(has_left))
    def _():
        recv_l[...] = jnp.zeros_like(recv_l)
        hg_recv_l[...] = jnp.zeros_like(hg_recv_l)

    @pl.when(jnp.logical_not(has_right))
    def _():
        recv_r[...] = jnp.zeros_like(recv_r)
        hg_recv_r[...] = jnp.zeros_like(hg_recv_r)

    pl.semaphore_wait(barrier, nf - 1 + has_left.astype(jnp.int32) + has_right.astype(jnp.int32))

    def doc_copy(s):
        return pltpu.make_async_remote_copy(
            doc_ref, docs_ref.at[me], dg_send.at[s], dg_recv.at[s],
            device_id=(lax.rem(me + 1 + s, nf), z), device_id_type=MESH)

    def row_copy(s):
        return pltpu.make_async_remote_copy(
            normed_ref, rows_ref.at[me], ag_send.at[s], ag_recv.at[s],
            device_id=(lax.rem(me + 1 + s, nf), z), device_id_type=MESH)

    def start_gather(s, c):
        doc_copy(s).start()
        return c

    lax.fori_loop(0, nf - 1, start_gather, 0)

    def start_rows(s, c):
        row_copy(s).start()
        return c

    lax.fori_loop(0, nf - 1, start_rows, 0)

    tokens = seg_ref.shape[1]
    match = (seg_ref[...] == lax.broadcasted_iota(jnp.int32, (docs, tokens), 0)).astype(F32)
    counts = jnp.sum(match, axis=1, keepdims=True)
    onehot = match.astype(BF16)

    def wait_docs(s, c):
        doc_copy(s).wait()
        return c

    lax.fori_loop(0, nf - 1, wait_docs, 0)
    flat = docs_ref[...].reshape(nf * piece_rows, 128)
    row = lax.broadcasted_iota(jnp.int32, (docs, nf * piece_rows), 0)
    col = lax.broadcasted_iota(jnp.int32, (docs, nf * piece_rows), 1)
    base = (row // doc_rows) * piece_rows + row % doc_rows
    pieces = []
    for i in range(feats // 128):
        pick = (col == base + i * doc_rows).astype(F32).astype(BF16)
        pieces.append(jnp.dot(pick, flat, preferred_element_type=F32))
    per_doc = (jnp.concatenate(pieces, axis=1) / counts).astype(BF16)

    loads[0].wait()
    hg_own[...] = lax.dot_general(per_doc, wd_ref[...], NT, preferred_element_type=F32)

    def hg_copy(right):
        return pltpu.make_async_remote_copy(
            hg_send_r if right else hg_send_l, hg_recv_l if right else hg_recv_r,
            hg_sems.at[0 if right else 1], hg_sems.at[2 if right else 3],
            device_id=(me, z + 1 if right else z - 1), device_id_type=MESH)

    def hg_pass(right):
        gets, sends = (has_left, has_right) if right else (has_right, has_left)
        source, out = (hg_recv_l, hg_send_r) if right else (hg_recv_r, hg_send_l)

        @pl.when(gets)
        def _():
            hg_copy(right).wait_recv()

        @pl.when(sends)
        def _():
            out[...] = (hg_own[...] + source[...].astype(F32)).astype(wire)
            hg_copy(right).start()

    def chain_copy(right, s, q):
        b = lax.rem(me + 1 + s, nf)
        return pltpu.make_async_remote_copy(
            (send_r if right else send_l).at[b, q], (recv_l if right else recv_r).at[b, q],
            (r_send if right else l_send).at[s, q], (r_recv if right else l_recv).at[s, q],
            device_id=(me, z + 1 if right else z - 1), device_id_type=MESH)

    def chain_pass(right, s):
        b = lax.rem(me + 1 + s, nf)
        gets, sends = (has_left, has_right) if right else (has_right, has_left)
        source, out = (recv_l, send_r) if right else (recv_r, send_l)
        for q in range(2):
            @pl.when(gets)
            def _():
                chain_copy(right, s, q).wait_recv()

            @pl.when(sends)
            def _():
                out[b, q] = (own_ref[b, q] + source[b, q].astype(F32)).astype(wire)
                chain_copy(right, s, q).start()

    def near(s):
        @pl.when(low_half)
        def _():
            chain_pass(True, s)

        @pl.when(jnp.logical_not(low_half))
        def _():
            chain_pass(False, s)

    def far(s):
        @pl.when(low_half)
        def _():
            chain_pass(False, s)

        @pl.when(jnp.logical_not(low_half))
        def _():
            chain_pass(True, s)

    def wait_rows(s, c):
        row_copy(s).wait()
        return c

    lax.fori_loop(0, nf - 1, wait_rows, 0)
    for load in loads[1:]:
        load.wait()

    def project(k, c):
        fs = pl.ds(pl.multiple_of(k * ft, ft), ft)
        rows = rows_ref[...].reshape(nf * t, feats)
        for q, w in enumerate((wg_ref, wu_ref)):
            part = jnp.dot(rows, w[:, fs], preferred_element_type=F32)
            own_ref[:, q, :, fs] = part.reshape(nf, t, ft)
        return c

    lax.fori_loop(0, width // ft, project, 0)

    at_end = jnp.logical_or(z == 0, z == ns - 1)

    @pl.when(low_half)
    def _():
        hg_pass(True)

    @pl.when(jnp.logical_not(low_half))
    def _():
        hg_pass(False)

    @pl.when(at_end)
    def _():
        def ahead(s, c):
            near(s)
            return c

        lax.fori_loop(0, nf, ahead, 0)

    rows_out[...] = rows_ref[...].reshape(nf * t, feats)
    og_ref[...] = lax.dot_general(onehot, per_doc, TN, preferred_element_type=F32).astype(BF16)

    def rs_copy(s):
        return pltpu.make_async_remote_copy(
            rs_send.at[s], rs_recv.at[s], rs_send_sems.at[s], rs_recv_sems.at[s],
            device_id=(lax.rem(me + 1 + s, nf), z), device_id_type=MESH)

    def work(s):
        b = lax.rem(me + 1 + s, nf)
        rs = pl.ds(pl.multiple_of(b * t, t), t)
        for k in range(width // ft):
            fs = slice(k * ft, (k + 1) * ft)
            gate, up = (
                own_ref[b, q, :, fs] + recv_l[b, q, :, fs].astype(F32) + recv_r[b, q, :, fs].astype(F32)
                for q in range(2)
            )
            grad = hg_tok[b, :, fs]
            sig = jax.nn.sigmoid(gate)
            silu = gate * sig
            hid_ref[rs, fs] = (silu * up).astype(BF16)
            gg_ref[rs, fs] = (grad * up * sig * (1.0 + gate * (1.0 - sig))).astype(BF16)
            ug_ref[rs, fs] = (grad * silu).astype(BF16)
        out = jnp.dot(hid_ref[rs, :], wd_ref[...], preferred_element_type=F32)
        back = lax.dot_general(gg_ref[rs, :], wg_ref[...], NT, preferred_element_type=F32)
        back = back + lax.dot_general(ug_ref[rs, :], wu_ref[...], NT, preferred_element_type=F32)

        @pl.when(s < nf - 1)
        def _():
            rs_send[s, 0] = out.astype(BF16)
            rs_send[s, 1] = back.astype(BF16)
            rs_copy(s).start()

        @pl.when(s == nf - 1)
        def _():
            mine_ref[0] = out
            mine_ref[1] = back

    def step(s, c):
        @pl.when(jnp.logical_and(s < nf, jnp.logical_not(at_end)))
        def _():
            near(s)

        @pl.when(s == 1)
        def _():
            @pl.when(low_half)
            def _():
                hg_pass(False)

            @pl.when(jnp.logical_not(low_half))
            def _():
                hg_pass(True)

            total = hg_own[...] + hg_recv_l[...].astype(F32) + hg_recv_r[...].astype(F32)
            high = total.astype(BF16)
            low = (total - high.astype(F32)).astype(BF16)
            spread = lax.dot_general(onehot, high, TN, preferred_element_type=F32)
            spread = spread + lax.dot_general(onehot, low, TN, preferred_element_type=F32)
            hg_tok[...] = spread.reshape(nf, t, width)

        @pl.when(s >= 1)
        def _():
            far(s - 1)
            work(s - 1)

        return c

    lax.fori_loop(0, nf + 1, step, 0)

    def collect(s, c):
        rs_copy(s).wait()
        for q in range(2):
            mine_ref[q] = mine_ref[q] + rs_recv[s, q].astype(F32)
        return c

    lax.fori_loop(0, nf - 1, collect, 0)
    layer_ref[...] = (normed_ref[...].astype(F32) + mine_ref[0]).astype(BF16)
    mine = pl.ds(pl.multiple_of(me * t, t), t)
    input_ref[...] = (og_ref[mine, :].astype(F32) + mine_ref[1]).astype(BF16)

    def drain(right):
        hg_copy(right).wait_send()

        def sent(s, c):
            for q in range(2):
                chain_copy(right, s, q).wait_send()
            return c

        lax.fori_loop(0, nf, sent, 0)

    @pl.when(has_right)
    def _():
        drain(True)

    @pl.when(has_left)
    def _():
        drain(False)


def grads_kernel(rows_ref, og_ref, hid_ref, gg_ref, ug_ref, gate_ref, up_ref, down_ref, rows_t):
    @pl.when(pl.program_id(0) == 0)
    def _():
        rows_t[...] = rows_ref[...].T

    gate_ref[...] = jnp.dot(rows_t[...], gg_ref[...], preferred_element_type=F32)
    up_ref[...] = jnp.dot(rows_t[...], ug_ref[...], preferred_element_type=F32)
    down_ref[...] = lax.dot_general(hid_ref[...], og_ref[...], TN, preferred_element_type=F32)


def body(nf, ns, normed, doc_grads, segment_ids, w_gate, w_up, w_down):
    t, feats = normed.shape
    width = w_gate.shape[1]
    doc_rows = doc_grads.shape[0]
    docs, tokens = doc_rows * nf, t * nf
    wire = BF16 if ns <= 4 else F32
    parts = feats // 128
    pieces = doc_grads.reshape(doc_rows, parts, 128).swapaxes(0, 1).reshape(doc_rows * parts, 128)
    piece_rows = -(-doc_rows * parts // 16) * 16
    pieces = jnp.pad(pieces, ((0, piece_rows - doc_rows * parts), (0, 0)))

    vmem = pl.BlockSpec(memory_space=pltpu.VMEM)
    hbm = pl.BlockSpec(memory_space=pl.ANY)
    dma = pltpu.SemaphoreType.DMA
    shape = jax.ShapeDtypeStruct
    layer_out, input_grad, rows, out_grad, hidden, gate_grad, up_grad = pl.pallas_call(
        functools.partial(encoder_kernel, nf, ns, docs, piece_rows, doc_rows),
        out_shape=[
            shape((t, feats), BF16), shape((t, feats), BF16),
            shape((tokens, feats), BF16), shape((tokens, feats), BF16),
            shape((tokens, width), BF16), shape((tokens, width), BF16), shape((tokens, width), BF16),
        ],
        in_specs=[vmem, vmem, vmem, hbm, hbm, hbm],
        out_specs=[vmem] * 7,
        scratch_shapes=[
            pltpu.VMEM(w_gate.shape, BF16), pltpu.VMEM(w_up.shape, BF16), pltpu.VMEM(w_down.shape, BF16),
            pltpu.VMEM((nf, t, feats), BF16), pltpu.VMEM((nf, piece_rows, 128), BF16),
            pltpu.VMEM((nf, 2, t, width), F32),
            *[pltpu.VMEM((nf, 2, t, width), wire)] * 4,
            pltpu.VMEM((docs, width), F32),
            *[pltpu.VMEM((docs, width), wire)] * 4,
            pltpu.VMEM((nf, t, width), F32),
            pltpu.VMEM((nf - 1, 2, t, feats), BF16), pltpu.VMEM((nf - 1, 2, t, feats), BF16),
            pltpu.VMEM((2, t, feats), F32),
            dma((3,)), dma((nf - 1,)), dma((nf - 1,)), dma((nf - 1,)), dma((nf - 1,)),
            dma((nf, 2)), dma((nf, 2)), dma((nf, 2)), dma((nf, 2)), dma((4,)),
            dma((nf - 1,)), dma((nf - 1,)),
        ],
        compiler_params=pltpu.CompilerParams(
            collective_id=0, has_side_effects=True, vmem_limit_bytes=VMEM_LIMIT),
    )(normed, pieces, segment_ids.reshape(1, tokens), w_gate, w_up, w_down)

    ft = tile_of(width)
    whole = pl.BlockSpec((tokens, feats), lambda k: (0, 0))
    columns = pl.BlockSpec((tokens, ft), lambda k: (0, k))
    grad_gate, grad_up, grad_down = pl.pallas_call(
        grads_kernel,
        grid=(width // ft,),
        out_shape=[shape((feats, width), F32), shape((feats, width), F32), shape((width, feats), F32)],
        in_specs=[whole, whole, columns, columns, columns],
        out_specs=[
            pl.BlockSpec((feats, ft), lambda k: (0, k)),
            pl.BlockSpec((feats, ft), lambda k: (0, k)),
            pl.BlockSpec((ft, feats), lambda k: (k, 0)),
        ],
        scratch_shapes=[pltpu.VMEM((feats, tokens), BF16)],
        compiler_params=pltpu.CompilerParams(vmem_limit_bytes=VMEM_LIMIT),
    )(rows, out_grad, hidden, gate_grad, up_grad)
    return (layer_out, input_grad, grad_gate, grad_up, grad_down)


def solution(mesh):
    rows, cols = P("fsdp", "seq"), P("seq", "fsdp")
    return jax.shard_map(
        functools.partial(body, mesh.shape["fsdp"], mesh.shape["seq"]),
        mesh=mesh,
        in_specs=(rows, rows, P(), cols, cols, rows),
        out_specs=(rows, rows, cols, cols, rows),
        check_vma=False,
    )
```

```python
import functools

import jax
import jax.numpy as jnp
from jax import lax
from jax.experimental import pallas as pl
from jax.experimental.pallas import tpu as pltpu
from jax.sharding import PartitionSpec as P

MESH = pl.DeviceIdType.MESH
BF16, F32 = jnp.bfloat16, jnp.float32
VMEM_LIMIT = 50 * 1024 * 1024
GRADS_LIMIT = 20 * 1024 * 1024
NT = (((1,), (1,)), ((), ()))
TN = (((0,), (0,)), ((), ()))


def tile_of(width):
    return 256 if width % 256 == 0 else 128


def encoder_kernel(
    nf, ns, docs, piece_rows, doc_rows,
    normed_ref, doc_ref, seg_hbm, wg_hbm, wu_hbm, wd_hbm,
    layer_ref, input_ref, rows_out, og_ref, hid_ref, gg_ref, ug_ref,
    wg_ref, wu_ref, wd_ref, rows_ref, docs_ref, own_ref, recv_l, recv_r, send_l, send_r,
    hg_own, hg_recv_l, hg_recv_r, hg_send_l, hg_send_r, hg_tok, rs_send, rs_recv, mine_ref,
    seg_ref, og_nat,
    load_sems, ag_send, ag_recv, dg_send, dg_recv,
    r_send, r_recv, l_send, l_recv, hg_sems, rs_send_sems, rs_recv_sems,
):
    me, z = lax.axis_index("fsdp"), lax.axis_index("seq")
    t = normed_ref.shape[0]
    width = wg_ref.shape[1]
    feats = normed_ref.shape[1]
    ft = tile_of(width)
    has_left, has_right = z > 0, z < ns - 1
    low_half = z < ns // 2
    wire = send_l.dtype

    loads = [
        pltpu.make_async_copy(src, dst, load_sems.at[k])
        for k, (src, dst) in enumerate((
            (normed_ref, rows_ref.at[nf - 1]), (wg_hbm, wg_ref), (wu_hbm, wu_ref),
            (doc_ref, docs_ref.at[me]), (seg_hbm, seg_ref), (wd_hbm, wd_ref)))
    ]
    for load in loads:
        load.start()

    barrier = pltpu.get_barrier_semaphore()

    def greet(s, c):
        pl.semaphore_signal(barrier, inc=1, device_id=(lax.rem(me + 1 + s, nf), z), device_id_type=MESH)
        return c

    lax.fori_loop(0, nf - 1, greet, 0)

    @pl.when(has_left)
    def _():
        pl.semaphore_signal(barrier, inc=1, device_id=(me, z - 1), device_id_type=MESH)

    @pl.when(has_right)
    def _():
        pl.semaphore_signal(barrier, inc=1, device_id=(me, z + 1), device_id_type=MESH)

    @pl.when(jnp.logical_not(has_left))
    def _():
        recv_l[...] = jnp.zeros_like(recv_l)
        hg_recv_l[...] = jnp.zeros_like(hg_recv_l)

    @pl.when(jnp.logical_not(has_right))
    def _():
        recv_r[...] = jnp.zeros_like(recv_r)
        hg_recv_r[...] = jnp.zeros_like(hg_recv_r)

    pl.semaphore_wait(barrier, nf - 1 + has_left.astype(jnp.int32) + has_right.astype(jnp.int32))

    def doc_copy(s):
        return pltpu.make_async_remote_copy(
            doc_ref, docs_ref.at[me], dg_send.at[s], dg_recv.at[s],
            device_id=(lax.rem(me + 1 + s, nf), z), device_id_type=MESH)

    def row_copy(s):
        return pltpu.make_async_remote_copy(
            normed_ref, rows_ref.at[s], ag_send.at[s], ag_recv.at[s],
            device_id=(lax.rem(me - 1 - s + nf, nf), z), device_id_type=MESH)

    def start_gather(s, c):
        doc_copy(s).start()
        return c

    half = nf // 2

    def start_rows(s, c):
        row_copy(s).start()
        return c

    lax.fori_loop(0, half, start_rows, 0)
    lax.fori_loop(0, nf - 1, start_gather, 0)
    lax.fori_loop(half, nf - 1, start_rows, 0)

    def hg_copy(right):
        return pltpu.make_async_remote_copy(
            hg_send_r if right else hg_send_l, hg_recv_l if right else hg_recv_r,
            hg_sems.at[0 if right else 1], hg_sems.at[2 if right else 3],
            device_id=(me, z + 1 if right else z - 1), device_id_type=MESH)

    def hg_pass(right):
        gets, sends = (has_left, has_right) if right else (has_right, has_left)
        source, out = (hg_recv_l, hg_send_r) if right else (hg_recv_r, hg_send_l)

        @pl.when(gets)
        def _():
            hg_copy(right).wait_recv()

        @pl.when(sends)
        def _():
            out[...] = (hg_own[...] + source[...].astype(F32)).astype(wire)
            hg_copy(right).start()

    def chain_copy(right, s, q):
        return pltpu.make_async_remote_copy(
            (send_r if right else send_l).at[s, q], (recv_l if right else recv_r).at[s, q],
            (r_send if right else l_send).at[s, q], (r_recv if right else l_recv).at[s, q],
            device_id=(me, z + 1 if right else z - 1), device_id_type=MESH)

    def chain_pass(right, s):
        gets, sends = (has_left, has_right) if right else (has_right, has_left)
        source, out = (recv_l, send_r) if right else (recv_r, send_l)
        for q in range(2):
            @pl.when(gets)
            def _():
                chain_copy(right, s, q).wait_recv()

            @pl.when(sends)
            def _():
                out[s, q] = (own_ref[s, q] + source[s, q].astype(F32)).astype(wire)
                chain_copy(right, s, q).start()

    def near(s):
        @pl.when(low_half)
        def _():
            chain_pass(True, s)

        @pl.when(jnp.logical_not(low_half))
        def _():
            chain_pass(False, s)

    def far(s):
        @pl.when(low_half)
        def _():
            chain_pass(False, s)

        @pl.when(jnp.logical_not(low_half))
        def _():
            chain_pass(True, s)

    def wait_rows(s, c):
        row_copy(s).wait()
        return c

    def project(first, last):
        def columns(k, c):
            fs = pl.ds(pl.multiple_of(k * ft, ft), ft)
            rows = rows_ref[first:last].reshape((last - first) * t, feats)
            for q, w in enumerate((wg_ref, wu_ref)):
                part = jnp.dot(rows, w[:, fs], preferred_element_type=F32)
                own_ref[first:last, q, :, fs] = part.reshape(last - first, t, ft)
            return c

        lax.fori_loop(0, width // ft, columns, 0)

    at_end = jnp.logical_or(z == 0, z == ns - 1)

    def ahead(first, last):
        @pl.when(at_end)
        def _():
            def one(s, c):
                near(s)
                return c

            lax.fori_loop(first, last, one, 0)

    def hg_near():
        @pl.when(low_half)
        def _():
            hg_pass(True)

        @pl.when(jnp.logical_not(low_half))
        def _():
            hg_pass(False)

    lax.fori_loop(0, half, wait_rows, 0)
    loads[1].wait()
    loads[2].wait()
    project(0, half)
    ahead(0, 2)

    loads[4].wait()
    tokens = seg_ref.shape[1]
    match = (seg_ref[...] == lax.broadcasted_iota(jnp.int32, (docs, tokens), 0)).astype(F32)
    counts = jnp.sum(match, axis=1, keepdims=True)
    onehot = match.astype(BF16)

    def wait_docs(s, c):
        doc_copy(s).wait()
        return c

    lax.fori_loop(0, nf - 1, wait_docs, 0)
    loads[3].wait()
    flat = docs_ref[...].reshape(nf * piece_rows, 128)
    row = lax.broadcasted_iota(jnp.int32, (docs, nf * piece_rows), 0)
    col = lax.broadcasted_iota(jnp.int32, (docs, nf * piece_rows), 1)
    base = (row // doc_rows) * piece_rows + row % doc_rows
    pieces = []
    for i in range(feats // 128):
        pick = (col == base + i * doc_rows).astype(F32).astype(BF16)
        pieces.append(jnp.dot(pick, flat, preferred_element_type=F32))
    per_doc = (jnp.concatenate(pieces, axis=1) / counts).astype(BF16)

    loads[5].wait()
    hg_own[...] = lax.dot_general(per_doc, wd_ref[...], NT, preferred_element_type=F32)

    @pl.when(at_end)
    def _():
        hg_near()

    lax.fori_loop(half, nf - 1, wait_rows, 0)
    loads[0].wait()
    project(half, nf)
    ahead(2, nf)

    rows_out[...] = rows_ref[...].reshape(nf * t, feats).T
    out_grad = lax.dot_general(onehot, per_doc, TN, preferred_element_type=F32).astype(BF16)
    og_nat[...] = out_grad.reshape(nf, t, feats)

    def rs_copy(s):
        return pltpu.make_async_remote_copy(
            rs_send.at[s], rs_recv.at[s], rs_send_sems.at[s], rs_recv_sems.at[s],
            device_id=(lax.rem(me + 1 + s, nf), z), device_id_type=MESH)

    def work(s):
        b = lax.rem(me + 1 + s, nf)
        rs = pl.ds(pl.multiple_of(s * t, t), t)
        og_ref[rs, :] = og_nat[b]
        for k in range(width // ft):
            fs = slice(k * ft, (k + 1) * ft)
            gate, up = (
                own_ref[s, q, :, fs] + recv_l[s, q, :, fs].astype(F32) + recv_r[s, q, :, fs].astype(F32)
                for q in range(2)
            )
            grad = hg_tok[b, :, fs]
            sig = jax.nn.sigmoid(gate)
            silu = gate * sig
            hid_ref[rs, fs] = (silu * up).astype(BF16)
            gg_ref[rs, fs] = (grad * up * sig * (1.0 + gate * (1.0 - sig))).astype(BF16)
            ug_ref[rs, fs] = (grad * silu).astype(BF16)
        out = jnp.dot(hid_ref[rs, :], wd_ref[...], preferred_element_type=F32)
        back = lax.dot_general(gg_ref[rs, :], wg_ref[...], NT, preferred_element_type=F32)
        back = back + lax.dot_general(ug_ref[rs, :], wu_ref[...], NT, preferred_element_type=F32)

        @pl.when(s < nf - 1)
        def _():
            rs_send[s, 0] = out.astype(BF16)
            rs_send[s, 1] = back.astype(BF16)
            rs_copy(s).start()

        @pl.when(s == nf - 1)
        def _():
            mine_ref[0] = out
            mine_ref[1] = back

    def step(s, c):
        @pl.when(jnp.logical_and(s < nf, jnp.logical_not(at_end)))
        def _():
            near(s)

        @pl.when(s >= 1)
        def _():
            far(s - 1)

        @pl.when(jnp.logical_and(s == 2, jnp.logical_not(at_end)))
        def _():
            hg_near()

        @pl.when(s == 3)
        def _():
            @pl.when(low_half)
            def _():
                hg_pass(False)

            @pl.when(jnp.logical_not(low_half))
            def _():
                hg_pass(True)

            total = hg_own[...] + hg_recv_l[...].astype(F32) + hg_recv_r[...].astype(F32)
            high = total.astype(BF16)
            low = (total - high.astype(F32)).astype(BF16)
            spread = lax.dot_general(onehot, high, TN, preferred_element_type=F32)
            spread = spread + lax.dot_general(onehot, low, TN, preferred_element_type=F32)
            hg_tok[...] = spread.reshape(nf, t, width)

        def one(k, c):
            work(k)
            return c

        lax.fori_loop(jnp.where(s > 3, s - 1, 0), jnp.where(s >= 3, s, 0), one, 0)
        return c

    lax.fori_loop(0, nf + 1, step, 0)

    def collect(s, c):
        rs_copy(s).wait()
        for q in range(2):
            mine_ref[q] = mine_ref[q] + rs_recv[s, q].astype(F32)
        return c

    lax.fori_loop(0, nf - 1, collect, 0)
    layer_ref[...] = (rows_ref[nf - 1].astype(F32) + mine_ref[0]).astype(BF16)
    input_ref[...] = (og_nat[me].astype(F32) + mine_ref[1]).astype(BF16)

    def drain(right):
        hg_copy(right).wait_send()

        def sent(s, c):
            for q in range(2):
                chain_copy(right, s, q).wait_send()
            return c

        lax.fori_loop(0, nf, sent, 0)

    @pl.when(has_right)
    def _():
        drain(True)

    @pl.when(has_left)
    def _():
        drain(False)


def grads_kernel(
    rows_t, og_ref, hid_ref, gg_ref, ug_ref, layer_in, input_in,
    layer_ref, input_ref, gate_ref, up_ref, down_ref,
):
    @pl.when(pl.program_id(0) == 0)
    def _():
        layer_ref[...] = layer_in[...]
        input_ref[...] = input_in[...]

    gate_ref[...] = jnp.dot(rows_t[...], gg_ref[...], preferred_element_type=F32)
    up_ref[...] = jnp.dot(rows_t[...], ug_ref[...], preferred_element_type=F32)
    down_ref[...] = lax.dot_general(hid_ref[...], og_ref[...], TN, preferred_element_type=F32)


def body(nf, ns, normed, doc_grads, segment_ids, w_gate, w_up, w_down):
    t, feats = normed.shape
    width = w_gate.shape[1]
    doc_rows = doc_grads.shape[0]
    docs, tokens = doc_rows * nf, t * nf
    wire = BF16 if ns <= 4 else F32
    parts = feats // 128
    pieces = doc_grads.reshape(doc_rows, parts, 128).swapaxes(0, 1).reshape(doc_rows * parts, 128)
    piece_rows = -(-doc_rows * parts // 16) * 16
    pieces = jnp.pad(pieces, ((0, piece_rows - doc_rows * parts), (0, 0)))

    vmem = pl.BlockSpec(memory_space=pltpu.VMEM)
    hbm = pl.BlockSpec(memory_space=pltpu.HBM)
    dma = pltpu.SemaphoreType.DMA
    shape = jax.ShapeDtypeStruct
    layer_part, input_part, rows_t, out_grad, hidden, gate_grad, up_grad = pl.pallas_call(
        functools.partial(encoder_kernel, nf, ns, docs, piece_rows, doc_rows),
        out_shape=[
            shape((t, feats), BF16), shape((t, feats), BF16),
            shape((feats, tokens), BF16), shape((tokens, feats), BF16),
            shape((tokens, width), BF16), shape((tokens, width), BF16), shape((tokens, width), BF16),
        ],
        in_specs=[hbm] * 6,
        out_specs=[vmem] * 7,
        scratch_shapes=[
            pltpu.VMEM(w_gate.shape, BF16), pltpu.VMEM(w_up.shape, BF16), pltpu.VMEM(w_down.shape, BF16),
            pltpu.VMEM((nf, t, feats), BF16), pltpu.VMEM((nf, piece_rows, 128), BF16),
            pltpu.VMEM((nf, 2, t, width), F32),
            *[pltpu.VMEM((nf, 2, t, width), wire)] * 4,
            pltpu.VMEM((docs, width), F32),
            *[pltpu.VMEM((docs, width), wire)] * 4,
            pltpu.VMEM((nf, t, width), F32),
            pltpu.VMEM((nf - 1, 2, t, feats), BF16), pltpu.VMEM((nf - 1, 2, t, feats), BF16),
            pltpu.VMEM((2, t, feats), F32),
            pltpu.VMEM((1, tokens), jnp.int32), pltpu.VMEM((nf, t, feats), BF16),
            dma((6,)), dma((nf - 1,)), dma((nf - 1,)), dma((nf - 1,)), dma((nf - 1,)),
            dma((nf, 2)), dma((nf, 2)), dma((nf, 2)), dma((nf, 2)), dma((4,)),
            dma((nf - 1,)), dma((nf - 1,)),
        ],
        compiler_params=pltpu.CompilerParams(
            collective_id=0, has_side_effects=True, vmem_limit_bytes=VMEM_LIMIT),
    )(normed, pieces, segment_ids.reshape(1, tokens), w_gate, w_up, w_down)

    ft = tile_of(width)
    whole = pl.BlockSpec((tokens, feats), lambda k: (0, 0))
    columns = pl.BlockSpec((tokens, ft), lambda k: (0, k))
    own = pl.BlockSpec((t, feats), lambda k: (0, 0))
    layer_out, input_grad, grad_gate, grad_up, grad_down = pl.pallas_call(
        grads_kernel,
        grid=(width // ft,),
        out_shape=[
            shape((t, feats), BF16), shape((t, feats), BF16),
            shape((feats, width), F32), shape((feats, width), F32), shape((width, feats), F32),
        ],
        in_specs=[
            pl.BlockSpec((feats, tokens), lambda k: (0, 0)), whole, columns, columns, columns, own, own,
        ],
        out_specs=[
            own, own,
            pl.BlockSpec((feats, ft), lambda k: (0, k)),
            pl.BlockSpec((feats, ft), lambda k: (0, k)),
            pl.BlockSpec((ft, feats), lambda k: (k, 0)),
        ],
        compiler_params=pltpu.CompilerParams(vmem_limit_bytes=GRADS_LIMIT),
    )(rows_t, out_grad, hidden, gate_grad, up_grad, layer_part, input_part)
    return (layer_out, input_grad, grad_gate, grad_up, grad_down)


def solution(mesh):
    rows, cols = P("fsdp", "seq"), P("seq", "fsdp")
    return jax.shard_map(
        functools.partial(body, mesh.shape["fsdp"], mesh.shape["seq"]),
        mesh=mesh,
        in_specs=(rows, rows, P(), cols, cols, rows),
        out_specs=(rows, rows, cols, cols, rows),
        check_vma=False,
    )
```
